768 devices in a mesh: ri: 12 (over z), ao: 64 (over x, y, core).
Axes of the slice: x: 4, y: 8, z: 12, core: 2. Of those that a mesh axis runs over, the one named last changes fastest.
Arguments:
- three_center: bfloat16 [12, 512, 512, 256], P('ri', None, 'ao'), may hold values from -0.375 to 0.375
- occ_density: bfloat16 [12, 512, 512], P('ri'), may hold values from -0.25 to 0.25
- virt_density: bfloat16 [12, 512, 512], P('ri'), may hold values from -0.25 to 0.25
- pair_mask: int32 [12, 16, 16], P('ri'), may hold values 0 or 1
- occ_mask: int32 [12, 16, 16], P('ri'), may hold values 0 or 1
- virt_mask: int32 [12, 16, 16], P('ri'), may hold values 0 or 1
Outputs:
- response: float32 [256, 256], P('ao')
The draws below stay inside these ranges and needn't reach their ends.
All inputs are finite; a program needn't handle non-finite values. No bound on the sum of `pair_mask` or of `occ_mask` or of `virt_mask` on one device may be relied on, other than what follows from the above.
Results may differ from the reference program's by a relative error of at most 0.0041.
Values may be sent and summed in bfloat16 or wider, within the bound.
A program may use at most 32 MiB of HBM per device.

```python
import jax
import jax.numpy as jnp
from jax import lax

NP = 256
NA = 512
NMOL = 16
N_RI = 12


def place_ends(array, stream_key, low, high):
    dims = array.shape
    place = [jax.random.randint(jax.random.fold_in(stream_key, axis), (), 0, dims[axis]) for axis in range(len(dims))]
    array = array.at[tuple(place)].set(low)
    longest = dims.index(max(dims))
    place[longest] = (place[longest] + 1) % dims[longest]
    return array.at[tuple(place)].set(high)


def raised(result, stream_key, source, target, blocks, factor):
    owner, partner = [(jnp.arange(result.shape[axis_at]) // (result.shape[axis_at] // blocks)).reshape([-1 if axis == axis_at else 1 for axis in range(result.ndim)]) for axis_at in (source, target)]
    chosen = jax.random.permutation(stream_key, blocks)[partner]
    strong = (owner == chosen) | (owner == (partner + blocks // 2) % blocks)
    return jnp.where(strong, factor * result, result)


def steps_of(stream_key, extent, split, least, largest):
    gain = 1.0
    for position, blocks in split:
        draws = jax.random.uniform(jax.random.fold_in(jax.random.fold_in(stream_key, 6), position), (blocks,), jnp.float32, least / len(split), largest / len(split))
        gain = gain * jnp.repeat(jnp.exp(draws), extent[position] // blocks).reshape((-1,) + (1,) * (len(extent) - 1 - position))
    return gain


def centred(own_key, dims, deviation, reach, shards=(), dtype=jnp.bfloat16):
    factor_of = steps_of(own_key, dims, shards, -0.22, 0.18) if shards else 1.0
    array = jax.random.normal(own_key, dims, jnp.float32) * deviation * factor_of
    return jnp.minimum(jnp.maximum(array, -reach), reach).astype(dtype)


def heavy_noise(stream_key, dims, deviation, reach, pieces, heavy, dtype=jnp.bfloat16):
    array = deviation * jax.random.normal(stream_key, dims, jnp.float32)
    if pieces:
        array = array * steps_of(stream_key, dims, pieces, -0.22, 0.18)
    return jnp.clip(raised(array, jax.random.fold_in(stream_key, 3), *heavy), -reach, reach).astype(dtype)


def setup_inputs(seed: int = 0) -> dict:
    seeds = jax.random.split(jax.random.key(seed), 7)
    three_center = heavy_noise(seeds[0], (N_RI, NA, NA, NP), ((NA * NA * N_RI) ** -0.25), 0.375, ((0, 12), (2, 64)), (2, 3, 64, 4.0))
    occ_density = centred(seeds[1], (N_RI, NA, NA), NA ** -0.5, 0.25, ((0, 12),))
    virt_density = centred(seeds[2], (N_RI, NA, NA), NA ** -0.5, 0.25, ((0, 12),))
    pair_mask = place_ends((jax.random.randint(seeds[3], (N_RI, NMOL, NMOL), 0, 4) < 3).astype(jnp.int32), jax.random.fold_in(seeds[3], 1), 0, 1)
    occ_mask = place_ends((jax.random.randint(seeds[4], (N_RI, NMOL, NMOL), 0, 4) < 3).astype(jnp.int32), jax.random.fold_in(seeds[4], 1), 0, 1)
    virt_mask = place_ends((jax.random.randint(seeds[5], (N_RI, NMOL, NMOL), 0, 4) < 3).astype(jnp.int32), jax.random.fold_in(seeds[5], 1), 0, 1)
    return dict(three_center=three_center, occ_density=occ_density, virt_density=virt_density, pair_mask=pair_mask, occ_mask=occ_mask, virt_mask=virt_mask)


def broadcast_pairs(mask, block_width):
    full = jnp.repeat(jnp.repeat(mask, block_width, axis=0), block_width, axis=1)
    return full.astype(jnp.bfloat16)


def window(call_arguments):
    three_index_tensor, occupied_block, virtual_block, pair_flags, occupied_flags, virtual_flags = call_arguments
    block_width = three_index_tensor.shape[0] // pair_flags.shape[0]
    masked = three_index_tensor * broadcast_pairs(pair_flags, block_width)[:, :, None]
    occ_m = occupied_block * broadcast_pairs(occupied_flags, block_width)
    virtual_masked = virtual_block * broadcast_pairs(virtual_flags, block_width)
    first = jnp.einsum("lm,mnp->lnp", occ_m.astype(jnp.float32), masked.astype(jnp.float32)).astype(jnp.bfloat16)
    second = jnp.einsum("lnp,ns->lsp", first.astype(jnp.float32), virtual_masked.astype(jnp.float32)).astype(jnp.bfloat16)
    return jnp.einsum("lsp,slq->pq", second.astype(jnp.float32), masked.astype(jnp.float32))


def reference(three_center, occ_density, virt_density, pair_mask, occ_mask, virt_mask):
    parts = lax.map(window, (three_center, occ_density, virt_density, pair_mask, occ_mask, virt_mask))
    return jnp.sum(parts, axis=0)
```

```python
import functools

import jax
import jax.numpy as jnp
from jax import lax
from jax.experimental import pallas as pl
from jax.experimental.pallas import tpu as pltpu
from jax.sharding import PartitionSpec as P

MESH = pl.DeviceIdType.MESH
X, Y, C, Z = 4, 8, 2, 12
AO = X * Y * C
NA, NP, W, BLOCKS = 512, 256, 8, 16
HALF = 128
SLABS = NP // HALF
F32, BF16 = jnp.float32, jnp.bfloat16


def dot(a, b, ca=1, cb=0):
    return lax.dot_general(a, b, (((ca,), (cb,)), ((), ())), preferred_element_type=F32)


def masked_density(density, mask, own_row):
    spread = (
        lax.broadcasted_iota(jnp.int32, (NA, BLOCKS), 0) // (NA // BLOCKS)
        == lax.broadcasted_iota(jnp.int32, (NA, BLOCKS), 1)
    ).astype(F32).astype(BF16)
    flags = (mask.astype(F32) * own_row).astype(BF16)
    rows = dot(spread, flags).astype(BF16)
    return density * dot(rows, spread, 1, 1).astype(BF16)


def kernel(
    three_hbm, occ_hbm, virt_hbm, pair_ref, occ_mask_ref, virt_mask_ref, out_ref,
    three, occ, virt, flat, cols, snd, rcv, tall, wide, psnd, prcv, zsnd, zrcv,
    load_sem, ssem, rsem, psend_sem, psem, zsend_sem, zsem,
):
    me = lax.axis_index("ao")
    z = lax.axis_index("ri")
    x, y, c = me // (Y * C), (me // C) % Y, me % C

    loads = [
        pltpu.make_async_copy(three_hbm.at[0, :, :, pl.ds(0, HALF)], three.at[0], load_sem.at[0]),
        pltpu.make_async_copy(occ_hbm.at[0], occ, load_sem.at[2]),
        pltpu.make_async_copy(three_hbm.at[0, :, :, pl.ds(HALF, HALF)], three.at[1], load_sem.at[1]),
        pltpu.make_async_copy(virt_hbm.at[0], virt, load_sem.at[3]),
    ]
    for load in loads:
        load.start()

    barrier = pltpu.get_barrier_semaphore()

    def greet(k, _):
        pl.semaphore_signal(barrier, inc=1, device_id={"ao": lax.rem(me + k, AO)}, device_id_type=MESH)
        return 0

    def greet_z(k, _):
        pl.semaphore_signal(barrier, inc=1, device_id={"ri": lax.rem(z + k, Z)}, device_id_type=MESH)
        return 0

    lax.fori_loop(1, AO, greet, 0)
    lax.fori_loop(1, Z, greet_z, 0)

    own = (lax.broadcasted_iota(jnp.int32, (8, BLOCKS), 1) == me // (NA // BLOCKS // W)).astype(F32).astype(BF16)
    own_row = dot(own, pair_ref[0].astype(F32).astype(BF16), 1, 1)[0:1]

    loads[1].wait()
    occ[...] = masked_density(occ[...], occ_mask_ref[0], own_row)

    for h in range(SLABS):
        loads[2 * h].wait()
        flat[...] = three[h].astype(F32).reshape(NA * W, HALF)
        for k in range(W // 2):
            even = flat[pl.ds(2 * k, NA, stride=W), :]
            odd = flat[pl.ds(2 * k + 1, NA, stride=W), :]
            cols[h, k] = jnp.concatenate([even, odd], axis=1).astype(BF16)
            first = dot(occ[...], cols[h, k])
            pair = [first[:, i * HALF : (i + 1) * HALF].reshape(AO, W, HALF) for i in range(2)]
            snd[h, :, 2 * W * k : 2 * W * (k + 1), :] = jnp.concatenate(pair, axis=1).astype(BF16)

        if h == 0:
            pl.semaphore_wait(barrier, AO - 1 + Z - 1)

        place = x * C + c
        pltpu.make_async_copy(snd.at[h, me], rcv.at[h, y, place], rsem.at[h, 0]).start()

        def send(k, _):
            dy = (k // C) % Y
            tx, ty, tc = lax.rem(x + k // (Y * C), X), lax.rem(y + dy, Y), lax.rem(c + k, C)
            target = (tx * Y + ty) * C + tc
            pltpu.make_async_remote_copy(
                src_ref=snd.at[h, target],
                dst_ref=rcv.at[h, y, place],
                send_sem=ssem.at[h],
                recv_sem=rsem.at[h, dy],
                device_id={"ao": target},
                device_id_type=MESH,
            ).start()
            return 0

        lax.fori_loop(1, AO, send, 0)

    loads[3].wait()
    virt[...] = masked_density(virt[...], virt_mask_ref[0], own_row)
    for h in range(SLABS):
        for k in range(W // 2):
            other = dot(virt[...], cols[h, k])
            for i in range(2):
                tall[h, pl.ds(2 * k + i, NA, stride=W), :] = other[:, i * HALF : (i + 1) * HALF]

    def turn(ty, _):
        for h in range(SLABS):
            for tx in range(X):
                rows = pl.multiple_of((tx * Y + ty) * (C * W * W), C * W * W)
                block = tall[h, pl.ds(rows, C * W * W), :]
                wide[ty, h * HALF : (h + 1) * HALF, tx * C * W * W : (tx + 1) * C * W * W] = block.T.astype(BF16)
        return 0

    lax.fori_loop(0, Y, turn, 0)

    def window_sum():
        pltpu.make_async_copy(prcv, prcv, psem).wait()
        zsnd[...] = jnp.sum(prcv[...], axis=0)
        zrcv[z] = zsnd[...]

        def send(k, _):
            pltpu.make_async_remote_copy(
                src_ref=zsnd,
                dst_ref=zrcv.at[z],
                send_sem=zsend_sem,
                recv_sem=zsem,
                device_id={"ri": lax.rem(z + k, Z)},
                device_id_type=MESH,
            ).start()
            return 0

        lax.fori_loop(1, Z, send, 0)

    for h in range(SLABS):
        total = jnp.zeros((NP, HALF), F32)
        for step, dy in enumerate((0, 1, 7, 2, 6, 3, 5, 4)):
            sy = lax.rem(y + Y - dy, Y)
            pltpu.make_async_copy(rcv.at[h, sy], rcv.at[h, sy], rsem.at[h, dy]).wait()
            total += dot(wide[sy], rcv[h, sy].reshape(X * C * W * W, HALF))
            if h == 1 and step == 4:
                pl.when(x < X // 2)(window_sum)
        low = total[:HALF].T.reshape(AO // 4, 8, HALF)
        high = total[HALF:].T.reshape(AO // 4, 8, HALF)
        top = lax.broadcasted_iota(jnp.int32, low.shape, 1) < 4
        psnd[h, :, 0] = jnp.where(top, low, pltpu.roll(high, 4, 1))
        psnd[h, :, 1] = jnp.where(top, pltpu.roll(low, 4, 1), high)

        def send(k, _):
            rank = lax.rem(me + k, AO // 2)
            target = h * (AO // 2) + rank

            @pl.when(target == me)
            def _():
                pltpu.make_async_copy(psnd.at[h, rank // C, rank % C], prcv.at[me], psem).start()

            @pl.when(target != me)
            def _():
                pltpu.make_async_remote_copy(
                    src_ref=psnd.at[h, rank // C, rank % C],
                    dst_ref=prcv.at[me],
                    send_sem=psend_sem,
                    recv_sem=psem,
                    device_id={"ao": target},
                    device_id_type=MESH,
                ).start()

            return 0

        lax.fori_loop(0, AO // 2, send, 0)

    pl.when(x >= X // 2)(window_sum)
    pltpu.make_async_copy(zrcv.at[pl.ds(0, Z - 1)], zrcv.at[pl.ds(0, Z - 1)], zsem).wait()
    total = jnp.sum(zrcv[...], axis=0)
    out_ref[:, 0:HALF] = total[0:4]
    out_ref[:, HALF:NP] = total[4:8]

    for h in range(SLABS):
        pltpu.make_async_copy(snd.at[h, pl.ds(0, AO - 1)], snd.at[h, pl.ds(0, AO - 1)], ssem.at[h]).wait()
    pltpu.make_async_copy(prcv.at[pl.ds(0, AO - 1)], prcv.at[pl.ds(0, AO - 1)], psend_sem).wait()
    pltpu.make_async_copy(zrcv.at[pl.ds(0, Z - 1)], zrcv.at[pl.ds(0, Z - 1)], zsend_sem).wait()


def body(three_center, occ_density, virt_density, pair_mask, occ_mask, virt_mask):
    hbm = pl.BlockSpec(memory_space=pl.ANY)
    vmem = pl.BlockSpec(memory_space=pltpu.VMEM)
    dma = pltpu.SemaphoreType.DMA
    return pl.pallas_call(
        kernel,
        out_shape=jax.ShapeDtypeStruct((NP // AO, NP), F32),
        in_specs=[hbm, hbm, hbm, vmem, vmem, vmem],
        out_specs=vmem,
        scratch_shapes=[
            pltpu.VMEM((SLABS, NA, W, HALF), BF16),
            pltpu.VMEM((NA, NA), BF16),
            pltpu.VMEM((NA, NA), BF16),
            pltpu.VMEM((NA * W, HALF), F32),
            pltpu.VMEM((SLABS, W // 2, NA, 2 * HALF), BF16),
            pltpu.VMEM((SLABS, AO, W * W, HALF), BF16),
            pltpu.VMEM((SLABS, Y, X * C, W * W, HALF), BF16),
            pltpu.VMEM((SLABS, NA * W, HALF), F32),
            pltpu.VMEM((Y, NP, X * C * W * W), BF16),
            pltpu.VMEM((SLABS, AO // 4, C, 8, HALF), F32),
            pltpu.VMEM((AO, 8, HALF), F32),
            pltpu.VMEM((8, HALF), F32),
            pltpu.VMEM((Z, 8, HALF), F32),
            dma((4,)), dma((SLABS,)), dma((SLABS, Y)), dma, dma, dma, dma,
        ],
        compiler_params=pltpu.CompilerParams(
            collective_id=0, has_side_effects=True, vmem_limit_bytes=40 * 2**20
        ),
        name="response",
    )(three_center, occ_density, virt_density, pair_mask, occ_mask, virt_mask)


def solution(mesh):
    return jax.shard_map(
        body,
        mesh=mesh,
        in_specs=(
            P("ri", None, "ao", None),
            P("ri", None, None),
            P("ri", None, None),
            P("ri", None, None),
            P("ri", None, None),
            P("ri", None, None),
        ),
        out_specs=P("ao", None),
        check_vma=False,
    )
```

```python
import functools

import jax
import jax.numpy as jnp
from jax import lax
from jax.experimental import pallas as pl
from jax.experimental.pallas import tpu as pltpu
from jax.sharding import PartitionSpec as P

MESH = pl.DeviceIdType.MESH
X, Y, C, Z = 4, 8, 2, 12
AO = X * Y * C
CHIPS = X * Y
EARLY_SEND, EARLY_SUM = 5, -1
NA, NP, W, BLOCKS = 512, 256, 8, 16
HALF = 128
SLABS = NP // HALF
FAR_Y = (4, 3, 5, 2, 6, 1, 7, 0)
FAR_Z = (6, 5, 7, 4, 8, 3, 9, 2, 10, 1, 11)
F32, BF16 = jnp.float32, jnp.bfloat16


def dot(a, b, ca=1, cb=0):
    return lax.dot_general(a, b, (((ca,), (cb,)), ((), ())), preferred_element_type=F32)


def masked_density(density, mask, own_row):
    spread = (
        lax.broadcasted_iota(jnp.int32, (NA, BLOCKS), 0) // (NA // BLOCKS)
        == lax.broadcasted_iota(jnp.int32, (NA, BLOCKS), 1)
    ).astype(F32).astype(BF16)
    flags = (mask.astype(F32) * own_row).astype(BF16)
    rows = dot(spread, flags).astype(BF16)
    return density * dot(rows, spread, 1, 1).astype(BF16)


def kernel(
    three_hbm, occ_hbm, virt_hbm, pair_hbm, occ_mask_hbm, virt_mask_hbm, out_ref,
    masks, three, occ, virt, flat, cols, snd, rcv, tall, wide, psnd, pmate, psum, prcv, zsnd, zrcv,
    load_sem, ssem, rsem, mate_send, mate_sem, psend_sem, psem, zsend_sem, zsem,
):
    me = lax.axis_index("ao")
    z = lax.axis_index("ri")
    x, y, c = me // (Y * C), (me // C) % Y, me % C

    loads = [
        pltpu.make_async_copy(pair_hbm, masks.at[pl.ds(0, 1)], load_sem.at[4]),
        pltpu.make_async_copy(occ_mask_hbm, masks.at[pl.ds(1, 1)], load_sem.at[5]),
        pltpu.make_async_copy(virt_mask_hbm, masks.at[pl.ds(2, 1)], load_sem.at[6]),
        pltpu.make_async_copy(three_hbm.at[0, :, :, pl.ds(0, HALF)], three.at[0], load_sem.at[0]),
        pltpu.make_async_copy(occ_hbm.at[0], occ, load_sem.at[2]),
        pltpu.make_async_copy(three_hbm.at[0, :, :, pl.ds(HALF, HALF)], three.at[1], load_sem.at[1]),
        pltpu.make_async_copy(virt_hbm.at[0], virt, load_sem.at[3]),
    ]
    for load in loads:
        load.start()

    barrier = pltpu.get_barrier_semaphore()

    for dz in FAR_Z:
        pl.semaphore_signal(barrier, inc=1, device_id={"ri": lax.rem(z + dz, Z)}, device_id_type=MESH)
    for dy in FAR_Y:

        def greet(k, _):
            target = (lax.rem(x + k // C, X) * Y + lax.rem(y + dy, Y)) * C + lax.rem(c + k, C)
            pl.semaphore_signal(barrier, inc=1, device_id={"ao": target}, device_id_type=MESH)
            return 0

        lax.fori_loop(int(dy == 0), X * C, greet, 0)

    own = (lax.broadcasted_iota(jnp.int32, (8, BLOCKS), 1) == me // (NA // BLOCKS // W)).astype(F32).astype(BF16)
    for load in loads[:3]:
        load.wait()
    own_row = dot(own, masks[0].astype(F32).astype(BF16), 1, 1)[0:1]

    loads[4].wait()
    occ[...] = masked_density(occ[...], masks[1], own_row)

    for h in range(SLABS):
        loads[3 + 2 * h].wait()
        flat[...] = three[h].astype(F32).reshape(NA * W, HALF)
        for k in range(W // 2):
            even = flat[pl.ds(2 * k, NA, stride=W), :]
            odd = flat[pl.ds(2 * k + 1, NA, stride=W), :]
            cols[h, k] = jnp.concatenate([even, odd], axis=1).astype(BF16)
            first = dot(occ[...], cols[h, k])
            pair = [first[:, i * HALF : (i + 1) * HALF].reshape(AO, W, HALF) for i in range(2)]
            snd[h, :, 2 * W * k : 2 * W * (k + 1), :] = jnp.concatenate(pair, axis=1).astype(BF16)

        if h == 0:
            pl.semaphore_wait(barrier, AO - 1 + Z - 1)

        place = x * C + c
        pltpu.make_async_copy(snd.at[h, me], rcv.at[h, y, place], rsem.at[h, 0]).start()

        def send(k, _):
            dy = (k // C) % Y
            tx, ty, tc = lax.rem(x + k // (Y * C), X), lax.rem(y + dy, Y), lax.rem(c + k, C)
            target = (tx * Y + ty) * C + tc
            pltpu.make_async_remote_copy(
                src_ref=snd.at[h, target],
                dst_ref=rcv.at[h, y, place],
                send_sem=ssem.at[h],
                recv_sem=rsem.at[h, dy],
                device_id={"ao": target},
                device_id_type=MESH,
            ).start()
            return 0

        lax.fori_loop(1, AO, send, 0)

    loads[6].wait()
    virt[...] = masked_density(virt[...], masks[2], own_row)
    for h in range(SLABS):
        for k in range(W // 2):
            other = dot(virt[...], cols[h, k])
            for i in range(2):
                tall[h, pl.ds(2 * k + i, NA, stride=W), :] = other[:, i * HALF : (i + 1) * HALF]

    def turn(ty, _):
        for h in range(SLABS):
            for tx in range(X):
                rows = pl.multiple_of((tx * Y + ty) * (C * W * W), C * W * W)
                block = tall[h, pl.ds(rows, C * W * W), :]
                wide[ty, h * HALF : (h + 1) * HALF, tx * C * W * W : (tx + 1) * C * W * W] = block.T.astype(BF16)
        return 0

    lax.fori_loop(0, Y, turn, 0)

    chip = x * Y + y

    def chip_sum(h):
        part = pl.ds(h * CHIPS // SLABS, CHIPS // SLABS)
        copy = pltpu.make_async_remote_copy(
            src_ref=psnd.at[1 - c, part],
            dst_ref=pmate.at[part],
            send_sem=mate_send.at[h],
            recv_sem=mate_sem.at[h],
            device_id={"ao": me + 1 - 2 * c},
            device_id_type=MESH,
        )
        copy.start()
        copy.wait_recv()
        psum[part] = psnd[c, part] + pmate[part]
        return copy

    def plane_send(h):
        for dy in FAR_Y:
            for tx in range(h * X // SLABS, (h + 1) * X // SLABS):
                target = tx * Y + lax.rem(y + dy, Y)

                @pl.when(target != chip)
                def _():
                    pltpu.make_async_remote_copy(
                        src_ref=psum.at[target],
                        dst_ref=prcv.at[chip],
                        send_sem=psend_sem,
                        recv_sem=psem,
                        device_id={"ao": C * target + c},
                        device_id_type=MESH,
                    ).start()

    def window_sum():
        prcv[chip] = psum[chip]
        pltpu.make_async_copy(prcv.at[pl.ds(0, CHIPS - 1)], prcv.at[pl.ds(0, CHIPS - 1)], psem).wait()
        zsnd[...] = jnp.sum(prcv[...], axis=0)
        zrcv[z] = zsnd[...]
        for dz in FAR_Z:
            pltpu.make_async_remote_copy(
                src_ref=zsnd,
                dst_ref=zrcv.at[z],
                send_sem=zsend_sem,
                recv_sem=zsem,
                device_id={"ri": lax.rem(z + dz, Z)},
                device_id_type=MESH,
            ).start()

    mates = []
    for h in range(SLABS):
        total = jnp.zeros((NP, HALF), F32)
        for step, dy in enumerate((0, 1, 7, 2, 6, 3, 5, 4)):
            sy = lax.rem(y + Y - dy, Y)
            pltpu.make_async_copy(rcv.at[h, sy], rcv.at[h, sy], rsem.at[h, dy]).wait()
            total += dot(wide[sy], rcv[h, sy].reshape(X * C * W * W, HALF))
            if h == 1 and step == EARLY_SEND:
                plane_send(0)
            if h == 1 and step == EARLY_SUM:
                pl.when(x < X // 2)(window_sum)
        low = total[:HALF].T.reshape(CHIPS // SLABS, 8, HALF)
        high = total[HALF:].T.reshape(CHIPS // SLABS, 8, HALF)
        top = lax.broadcasted_iota(jnp.int32, low.shape, 1) < 4
        part = pl.ds(h * CHIPS // SLABS, CHIPS // SLABS)
        psnd[0, part] = jnp.where(top, low, pltpu.roll(high, 4, 1))
        psnd[1, part] = jnp.where(top, pltpu.roll(low, 4, 1), high)
        mates.append(chip_sum(h))

    plane_send(1)
    if EARLY_SUM < 0:
        window_sum()
    else:
        pl.when(x >= X // 2)(window_sum)
    pltpu.make_async_copy(zrcv.at[pl.ds(0, Z - 1)], zrcv.at[pl.ds(0, Z - 1)], zsem).wait()
    total = jnp.sum(zrcv[...], axis=0)
    out_ref[:, 0:HALF] = total[0:4]
    out_ref[:, HALF:NP] = total[4:8]

    for h in range(SLABS):
        pltpu.make_async_copy(snd.at[h, pl.ds(0, AO - 1)], snd.at[h, pl.ds(0, AO - 1)], ssem.at[h]).wait()
    for mate in mates:
        mate.wait_send()
    pltpu.make_async_copy(prcv.at[pl.ds(0, CHIPS - 1)], prcv.at[pl.ds(0, CHIPS - 1)], psend_sem).wait()
    pltpu.make_async_copy(zrcv.at[pl.ds(0, Z - 1)], zrcv.at[pl.ds(0, Z - 1)], zsend_sem).wait()


def body(three_center, occ_density, virt_density, pair_mask, occ_mask, virt_mask):
    hbm = pl.BlockSpec(memory_space=pl.ANY)
    vmem = pl.BlockSpec(memory_space=pltpu.VMEM)
    dma = pltpu.SemaphoreType.DMA
    return pl.pallas_call(
        kernel,
        out_shape=jax.ShapeDtypeStruct((NP // AO, NP), F32),
        in_specs=[hbm] * 6,
        out_specs=vmem,
        scratch_shapes=[
            pltpu.VMEM((3, BLOCKS, BLOCKS), jnp.int32),
            pltpu.VMEM((SLABS, NA, W, HALF), BF16),
            pltpu.VMEM((NA, NA), BF16),
            pltpu.VMEM((NA, NA), BF16),
            pltpu.VMEM((NA * W, HALF), F32),
            pltpu.VMEM((SLABS, W // 2, NA, 2 * HALF), BF16),
            pltpu.VMEM((SLABS, AO, W * W, HALF), BF16),
            pltpu.VMEM((SLABS, Y, X * C, W * W, HALF), BF16),
            pltpu.VMEM((SLABS, NA * W, HALF), F32),
            pltpu.VMEM((Y, NP, X * C * W * W), BF16),
            pltpu.VMEM((C, CHIPS, 8, HALF), F32),
            pltpu.VMEM((CHIPS, 8, HALF), F32),
            pltpu.VMEM((CHIPS, 8, HALF), F32),
            pltpu.VMEM((CHIPS, 8, HALF), F32),
            pltpu.VMEM((8, HALF), F32),
            pltpu.VMEM((Z, 8, HALF), F32),
            dma((7,)), dma((SLABS,)), dma((SLABS, Y)), dma((SLABS,)), dma((SLABS,)), dma, dma, dma, dma,
        ],
        compiler_params=pltpu.CompilerParams(
            collective_id=0, has_side_effects=True, vmem_limit_bytes=60 * 2**20
        ),
        name="response",
    )(three_center, occ_density, virt_density, pair_mask, occ_mask, virt_mask)


def solution(mesh):
    return jax.shard_map(
        body,
        mesh=mesh,
        in_specs=(
            P("ri", None, "ao", None),
            P("ri", None, None),
            P("ri", None, None),
            P("ri", None, None),
            P("ri", None, None),
            P("ri", None, None),
        ),
        out_specs=P("ao", None),
        check_vma=False,
    )
```

```python
import functools

import jax
import jax.numpy as jnp
from jax import lax
from jax.experimental import pallas as pl
from jax.experimental.pallas import tpu as pltpu
from jax.sharding import PartitionSpec as P

MESH = pl.DeviceIdType.MESH
X, Y, C, Z = 4, 8, 2, 12
AO = X * Y * C
CHIPS = X * Y
EARLY_SEND = 6
NA, NP, W, BLOCKS = 512, 256, 8, 16
HALF = 128
SLABS = NP // HALF
FAR_Y = (4, 3, 5, 2, 6, 1, 7, 0)
FAR_Z = (6, 5, 7, 4, 8, 3, 9, 2, 10, 1, 11)
PAIR_Y = (4, 1, 7, 2, 6, 3, 5, 0)
SETS = ((0, 0), (0, 1), (1, 0), (1, 1), (3, 0), (3, 1), (2, 0), (2, 1))
F32, BF16 = jnp.float32, jnp.bfloat16


def dot(a, b, ca=1, cb=0):
    return lax.dot_general(a, b, (((ca,), (cb,)), ((), ())), preferred_element_type=F32)


def masked_density(density, mask, own_row):
    spread = (
        lax.broadcasted_iota(jnp.int32, (NA, BLOCKS), 0) // (NA // BLOCKS)
        == lax.broadcasted_iota(jnp.int32, (NA, BLOCKS), 1)
    ).astype(F32).astype(BF16)
    flags = (mask.astype(F32) * own_row).astype(BF16)
    rows = dot(spread, flags).astype(BF16)
    return density * dot(rows, spread, 1, 1).astype(BF16)


def kernel(
    three_hbm, occ_hbm, virt_hbm, pair_hbm, occ_mask_hbm, virt_mask_hbm, out_ref,
    masks, three, occ, virt, flat, cols, snd, rcv, tall, wide, psnd, pmate, psum, prcv, zsnd, zrcv,
    load_sem, ssem, rsem, mate_send, mate_sem, psend_sem, psem, zsend_sem, zsem,
):
    me = lax.axis_index("ao")
    z = lax.axis_index("ri")
    x, y, c = me // (Y * C), (me // C) % Y, me % C

    barrier = pltpu.get_barrier_semaphore()

    for dz in FAR_Z:
        pl.semaphore_signal(barrier, inc=1, device_id={"ri": lax.rem(z + dz, Z)}, device_id_type=MESH)
    for dy in FAR_Y:

        def greet(k, _):
            target = (lax.rem(x + k // C, X) * Y + lax.rem(y + dy, Y)) * C + lax.rem(c + k, C)
            pl.semaphore_signal(barrier, inc=1, device_id={"ao": target}, device_id_type=MESH)
            return 0

        lax.fori_loop(int(dy == 0), X * C, greet, 0)

    loads = [
        pltpu.make_async_copy(pair_hbm, masks.at[pl.ds(0, 1)], load_sem.at[4]),
        pltpu.make_async_copy(occ_mask_hbm, masks.at[pl.ds(1, 1)], load_sem.at[5]),
        pltpu.make_async_copy(virt_mask_hbm, masks.at[pl.ds(2, 1)], load_sem.at[6]),
        pltpu.make_async_copy(three_hbm.at[0, :, :, pl.ds(0, HALF)], three.at[0], load_sem.at[0]),
        pltpu.make_async_copy(occ_hbm.at[0], occ, load_sem.at[2]),
        pltpu.make_async_copy(three_hbm.at[0, :, :, pl.ds(HALF, HALF)], three.at[1], load_sem.at[1]),
        pltpu.make_async_copy(virt_hbm.at[0], virt, load_sem.at[3]),
    ]
    for load in loads:
        load.start()

    own = (lax.broadcasted_iota(jnp.int32, (8, BLOCKS), 1) == me // (NA // BLOCKS // W)).astype(F32).astype(BF16)
    for load in loads[:3]:
        load.wait()
    own_row = dot(own, masks[0].astype(F32).astype(BF16), 1, 1)[0:1]

    loads[4].wait()
    occ[...] = masked_density(occ[...], masks[1], own_row)

    for h in range(SLABS):
        loads[3 + 2 * h].wait()
        flat[...] = three[h].astype(F32).reshape(NA * W, HALF)
        for k in range(W // 2):
            even = flat[pl.ds(2 * k, NA, stride=W), :]
            odd = flat[pl.ds(2 * k + 1, NA, stride=W), :]
            cols[h, k] = jnp.concatenate([even, odd], axis=1).astype(BF16)
            first = dot(occ[...], cols[h, k])
            pair = [first[:, i * HALF : (i + 1) * HALF].reshape(AO, W, HALF) for i in range(2)]
            snd[h, :, 2 * W * k : 2 * W * (k + 1), :] = jnp.concatenate(pair, axis=1).astype(BF16)

        if h == 0:
            pl.semaphore_wait(barrier, AO - 1 + Z - 1)

        own_set = x * C + c
        pltpu.make_async_copy(snd.at[h, me], rcv.at[h, own_set, y], rsem.at[h, 0]).start()
        for g, (dx, dc) in enumerate(SETS):
            for dy in PAIR_Y:
                if dx or dc or dy:
                    target = (lax.rem(x + dx, X) * Y + lax.rem(y + dy, Y)) * C + lax.rem(c + dc, C)
                    pltpu.make_async_remote_copy(
                        src_ref=snd.at[h, target],
                        dst_ref=rcv.at[h, own_set, y],
                        send_sem=ssem.at[h],
                        recv_sem=rsem.at[h, g],
                        device_id={"ao": target},
                        device_id_type=MESH,
                    ).start()

    loads[6].wait()
    virt[...] = masked_density(virt[...], masks[2], own_row)
    for h in range(SLABS):
        for k in range(W // 2):
            other = dot(virt[...], cols[h, k])
            for i in range(2):
                tall[h, pl.ds(2 * k + i, NA, stride=W), :] = other[:, i * HALF : (i + 1) * HALF]

    def turn(i, _):
        for h in range(SLABS):
            for tx in range(X):
                rows = pl.multiple_of((tx * Y + C * i) * (C * W * W), C * C * W * W)
                block = tall[h, pl.ds(rows, C * C * W * W), :].T.astype(BF16)
                for tc in range(C):
                    mine = [block[:, (C * j + tc) * W * W : (C * j + tc + 1) * W * W] for j in range(C)]
                    wide[tx * C + tc, h * HALF : (h + 1) * HALF, pl.ds(pl.multiple_of(i * HALF, HALF), HALF)] = jnp.concatenate(mine, axis=1)
        return 0

    lax.fori_loop(0, Y // C, turn, 0)

    chip = x * Y + y

    def mate_copy(h):
        part = pl.ds(h * CHIPS // SLABS, CHIPS // SLABS)
        return pltpu.make_async_remote_copy(
            src_ref=psnd.at[1 - c, part],
            dst_ref=pmate.at[part],
            send_sem=mate_send.at[h],
            recv_sem=mate_sem.at[h],
            device_id={"ao": me + 1 - 2 * c},
            device_id_type=MESH,
        )

    def chip_sum(h):
        part = pl.ds(h * CHIPS // SLABS, CHIPS // SLABS)
        mate_copy(h).wait_recv()
        psum[part] = psnd[c, part] + pmate[part]
        plane_send(h)

    def plane_send(h):
        for dy in FAR_Y:
            for tx in range(h * X // SLABS, (h + 1) * X // SLABS):
                target = tx * Y + lax.rem(y + dy, Y)

                @pl.when(target != chip)
                def _():
                    pltpu.make_async_remote_copy(
                        src_ref=psum.at[target],
                        dst_ref=prcv.at[chip],
                        send_sem=psend_sem,
                        recv_sem=psem,
                        device_id={"ao": C * target + c},
                        device_id_type=MESH,
                    ).start()

    def window_sum():
        prcv[chip] = psum[chip]
        pltpu.make_async_copy(prcv.at[pl.ds(0, CHIPS - 1)], prcv.at[pl.ds(0, CHIPS - 1)], psem).wait()
        zsnd[...] = jnp.sum(prcv[...], axis=0)
        zrcv[z] = zsnd[...]
        for dz in FAR_Z:
            pltpu.make_async_remote_copy(
                src_ref=zsnd,
                dst_ref=zrcv.at[z],
                send_sem=zsend_sem,
                recv_sem=zsem,
                device_id={"ri": lax.rem(z + dz, Z)},
                device_id_type=MESH,
            ).start()

    for h in range(SLABS):
        total = jnp.zeros((NP, HALF), F32)
        for g, (dx, dc) in enumerate(SETS):
            source = lax.rem(x + X - dx, X) * C + lax.rem(c + dc, C)
            pltpu.make_async_copy(rcv.at[h, source], rcv.at[h, source], rsem.at[h, g]).wait()
            total += dot(wide[source], rcv[h, source].reshape(Y * W * W, HALF))
            if h == 1 and g == EARLY_SEND:
                chip_sum(0)
        low = total[:HALF].T.reshape(CHIPS // SLABS, 8, HALF)
        high = total[HALF:].T.reshape(CHIPS // SLABS, 8, HALF)
        top = lax.broadcasted_iota(jnp.int32, low.shape, 1) < 4
        part = pl.ds(h * CHIPS // SLABS, CHIPS // SLABS)
        psnd[0, part] = jnp.where(top, low, pltpu.roll(high, 4, 1))
        psnd[1, part] = jnp.where(top, pltpu.roll(low, 4, 1), high)
        mate_copy(h).start()

    if EARLY_SEND == len(SETS):
        chip_sum(0)
    chip_sum(1)
    window_sum()
    pltpu.make_async_copy(zrcv.at[pl.ds(0, Z - 1)], zrcv.at[pl.ds(0, Z - 1)], zsem).wait()
    total = jnp.sum(zrcv[...], axis=0)
    out_ref[:, 0:HALF] = total[0:4]
    out_ref[:, HALF:NP] = total[4:8]

    for h in range(SLABS):
        pltpu.make_async_copy(snd.at[h, pl.ds(0, AO - 1)], snd.at[h, pl.ds(0, AO - 1)], ssem.at[h]).wait()
    for h in range(SLABS):
        mate_copy(h).wait_send()
    pltpu.make_async_copy(prcv.at[pl.ds(0, CHIPS - 1)], prcv.at[pl.ds(0, CHIPS - 1)], psend_sem).wait()
    pltpu.make_async_copy(zrcv.at[pl.ds(0, Z - 1)], zrcv.at[pl.ds(0, Z - 1)], zsend_sem).wait()


def body(three_center, occ_density, virt_density, pair_mask, occ_mask, virt_mask):
    hbm = pl.BlockSpec(memory_space=pl.ANY)
    vmem = pl.BlockSpec(memory_space=pltpu.VMEM)
    dma = pltpu.SemaphoreType.DMA
    return pl.pallas_call(
        kernel,
        out_shape=jax.ShapeDtypeStruct((NP // AO, NP), F32),
        in_specs=[hbm] * 6,
        out_specs=vmem,
        scratch_shapes=[
            pltpu.VMEM((3, BLOCKS, BLOCKS), jnp.int32),
            pltpu.VMEM((SLABS, NA, W, HALF), BF16),
            pltpu.VMEM((NA, NA), BF16),
            pltpu.VMEM((NA, NA), BF16),
            pltpu.VMEM((NA * W, HALF), F32),
            pltpu.VMEM((SLABS, W // 2, NA, 2 * HALF), BF16),
            pltpu.VMEM((SLABS, AO, W * W, HALF), BF16),
            pltpu.VMEM((SLABS, X * C, Y, W * W, HALF), BF16),
            pltpu.VMEM((SLABS, NA * W, HALF), F32),
            pltpu.VMEM((X * C, NP, Y * W * W), BF16),
            pltpu.VMEM((C, CHIPS, 8, HALF), F32),
            pltpu.VMEM((CHIPS, 8, HALF), F32),
            pltpu.VMEM((CHIPS, 8, HALF), F32),
            pltpu.VMEM((CHIPS, 8, HALF), F32),
            pltpu.VMEM((8, HALF), F32),
            pltpu.VMEM((Z, 8, HALF), F32),
            dma((7,)), dma((SLABS,)), dma((SLABS, len(SETS))), dma((SLABS,)), dma((SLABS,)), dma, dma, dma, dma,
        ],
        compiler_params=pltpu.CompilerParams(
            collective_id=0, has_side_effects=True, vmem_limit_bytes=60 * 2**20
        ),
        name="response",
    )(three_center, occ_density, virt_density, pair_mask, occ_mask, virt_mask)


def solution(mesh):
    return jax.shard_map(
        body,
        mesh=mesh,
        in_specs=(
            P("ri", None, "ao", None),
            P("ri", None, None),
            P("ri", None, None),
            P("ri", None, None),
            P("ri", None, None),
            P("ri", None, None),
        ),
        out_specs=P("ao", None),
        check_vma=False,
    )
```
